32 devices in a mesh: grp: 2 (over x), ref: 16 (over z, y, core).
Axes of the slice: x: 2, y: 2, z: 4, core: 2. Of those that a mesh axis runs over, the one named last changes fastest.
Arguments:
- references: bfloat16 [24576, 16384], P(('grp', 'ref')), parts along dimension 0
- noise: float32 [256, 16384], P('grp', 'ref'), parts along dimension 0
- init_idx: int32 [256], P('grp'), parts along dimension 0, may hold values from 0 to 12287
Outputs:
- paths: float32 [256, 16384], P('grp', 'ref'), parts along dimension 0
The draws below stay inside these ranges and needn't reach their ends.
There are 2 independent parts, one for each index of `grp`. The reference program is written for one: setup_inputs(seed, part) draws one part's arguments, and reference() takes and returns one part's arrays. A program takes and returns all parts, laid end to end along the dimension named above; each array names one. Nothing has to cross between parts.
All inputs are finite; a program needn't handle non-finite values.
Results may differ from the reference program's by a relative error of at most 0.0003.
Values may be sent and summed in bfloat16 or wider, within the bound.
A program may use at most 128 MiB of HBM per device.

```python
import math
import jax
import jax.numpy as jnp
from jax import lax

D = 16384
M = 128
STEPS = 2
REFS = 12288


def draw_references(key, part):
    key = jax.random.fold_in(key, 11)
    sign_key, load_key, rest_key = jax.random.split(key, 3)
    factor_signs = (2 * jax.random.randint(sign_key, (REFS, 16), 0, 2) - 1).astype(jnp.float32)
    loadings = jax.random.randint(load_key, (16, D), -3, 4).astype(jnp.float32)
    spread = 4.0
    residual_part = jax.random.normal(rest_key, (REFS, D), jnp.float32)
    shared_part = jnp.dot(factor_signs, loadings, precision=lax.Precision.HIGHEST)
    values = math.sqrt(0.75 / (16.0 * spread)) * shared_part + 0.5 * residual_part
    return values.astype(jnp.bfloat16)


def draw_noise(key, part):
    key = jax.random.fold_in(key, 12)
    values = jax.random.normal(key, (M, D), jnp.float32)
    return values


def touch_ends(array, rng, smallest, high):
    longest = array.shape.index(max(array.shape))
    spots = []
    for shift in (0, 1):
        where = [jax.random.randint(jax.random.fold_in(rng, axis), (), 0, length) for axis, length in enumerate(array.shape)]
        where[longest] = (where[longest] + shift) % array.shape[longest]
        spots.append(tuple(where))
    return array.at[spots[0]].set(smallest).at[spots[1]].set(high)


def setup_inputs(seed: int = 0, part: int = 0) -> dict:
    splits = jax.random.split(jax.random.key(seed), 4)
    part_keys = jax.random.split(jax.random.fold_in(splits[3], part), 4)
    return {
        "references": draw_references(jax.random.fold_in(jax.random.fold_in(splits[3], part), 71), part),
        "noise": draw_noise(jax.random.fold_in(jax.random.fold_in(splits[3], part), 71), part),
        "init_idx": touch_ends(jax.random.randint(part_keys[2], (M,), 0, REFS), jax.random.fold_in(part_keys[2], 1), 0, REFS - 1).astype(jnp.int32),
    }


SHARP = 7.0
STEP_RATE = 0.025


def reference(references, noise, init_idx):
    ref_sq = jnp.sum(jnp.square(references.astype(jnp.float32)), axis=1)
    scale = jnp.sum(ref_sq) / REFS
    paths = 0.6 * references[init_idx].astype(jnp.float32) + 0.8 * noise
    offdiag = 1.0 - jnp.eye(M, dtype=jnp.float32)
    for step in range(STEPS):
        pathb = paths.astype(jnp.bfloat16)
        gram = jnp.dot(pathb, pathb.T, preferred_element_type=jnp.float32)
        sq = jnp.diagonal(gram)
        scores = jnp.dot(pathb, references.T, preferred_element_type=jnp.float32)
        weights = jnp.exp(SHARP * (2.0 * scale - sq[:, None] - ref_sq[None, :] + 2.0 * scores) / scale)
        totals = jnp.sum(weights, axis=1)
        weightb = weights.astype(jnp.bfloat16)
        pulled = jnp.dot(weightb, references, preferred_element_type=jnp.float32)
        mutual = jnp.exp(SHARP * (2.0 * scale - sq[:, None] - sq[None, :] + 2.0 * gram) / scale) * offdiag
        mutual_sum = jnp.sum(mutual, axis=1)
        pushed = jnp.dot(mutual, paths, precision=lax.Precision.HIGHEST)
        paths = paths + (STEP_RATE / M) * (mutual_sum[:, None] * paths - pushed) - (STEP_RATE / REFS) * (totals[:, None] * paths - pulled)
    return paths
```

```python
import functools

import jax
import jax.numpy as jnp
from jax import lax
from jax.experimental import pallas as pl
from jax.experimental.pallas import tpu as pltpu
from jax.sharding import PartitionSpec as P

STEPS = 2
SHARP = 7.0
STEP_RATE = 0.025
MESH = pl.DeviceIdType.MESH
NT = (((1,), (1,)), ((), ()))


def kernel(
    n, idx_ref, noise_ref, refs_hbm, out_ref,
    refs, gath, sib_out, sib_in, ring_out, ring_in, part, paths, base,
    sq_acc, scores, gram, weightb, totals_out, totals_in,
    load_sem, ag_send, ag_recv, agsib_send, agsib_recv,
    rs_send, rs_recv, rssib_send, rssib_recv, ex_send, ex_recv,
):
    chips, half = n // 2, n // 4
    m, width = noise_ref.shape
    rows = refs.shape[0]
    mh = m // 2
    all_refs = rows * n
    me = lax.axis_index("ref")
    chip, core = me // 2, me % 2
    other = 1 - core

    if n == 16:
        ring = chip // 2 + (chip % 2) * (chips - 1 - 2 * (chip // 2))

        def chip_at(r):
            back = r // half
            return back * (2 * (chips - 1 - r) + 1) + (1 - back) * 2 * r
    else:
        ring = chip

        def chip_at(r):
            return r

    def at(r):
        return (r + chips) % chips

    def pos(r, c):
        return chip_at(r) * 2 + c

    right = pos(at(ring + 1), core)
    left = pos(at(ring - 1), core)
    sibling = chip * 2 + other
    toward = (right, left)

    def columns(r, c):
        return pl.multiple_of(pos(r, c) * width, width)

    def remote(src, dst, send, recv, dev):
        return pltpu.make_async_remote_copy(
            src_ref=src, dst_ref=dst, send_sem=send, recv_sem=recv,
            device_id={"ref": dev}, device_id_type=MESH,
        )

    def load(r, c):
        cols = pl.ds(columns(r, c), width)
        return pltpu.make_async_copy(
            refs_hbm.at[:, cols], refs.at[:, cols], load_sem.at[r * 2 + c]
        )

    stages = [half] + list(range(half - 1, 0, -1)) + [0]

    def targets(k):
        if k == 0 or k == half:
            return [at(ring + k)]
        return [at(ring + k), at(ring - k)]

    for k in stages:
        for t in targets(k):
            load(t, other).start()
            load(t, core).start()

    barrier = pltpu.get_barrier_semaphore()

    def greet(i, carry):
        pl.semaphore_signal(
            barrier, inc=1, device_id={"ref": (me + i) % n}, device_id_type=MESH
        )
        return carry

    lax.fori_loop(1, n, greet, 0)

    offset = idx_ref[...] - me * rows
    lanes = lax.broadcasted_iota(jnp.int32, (m, rows), 1)
    weightb[...] = (lanes == offset).astype(jnp.float32).astype(jnp.bfloat16)
    sq_acc[...] = jnp.zeros_like(sq_acc)
    eye = (
        lax.broadcasted_iota(jnp.int32, (m, m), 0) == lax.broadcasted_iota(jnp.int32, (m, m), 1)
    ).astype(jnp.float32)
    pl.semaphore_wait(barrier, n - 1)

    def partial(r, c):
        cols = pl.ds(columns(r, c), width)
        return jnp.dot(weightb[...], refs[:, cols], preferred_element_type=jnp.float32)

    def squares(r, c):
        start = columns(r, c)
        chunk = 64

        def body(i, carry):
            rs = pl.ds(pl.multiple_of(i * chunk, chunk), chunk)
            total = sq_acc[rs, :]
            for j in range(width // 128):
                x = refs[rs, pl.ds(pl.multiple_of(start + j * 128, 128), 128)].astype(jnp.float32)
                total = total + x * x
            sq_acc[rs, :] = total
            return carry

        lax.fori_loop(0, rows // chunk, body, 0)

    def rs_copy(d, p, k):
        piece = pl.ds(p * mh, mh)
        return remote(
            ring_out.at[d, k - 1, piece, :], ring_in.at[d, k - 1, piece, :],
            rs_send.at[d, p, k - 1], rs_recv.at[d, p, k - 1], toward[d],
        )

    def rs_sib(t):
        return remote(
            sib_out.at[t], sib_in.at[t], rssib_send.at[t], rssib_recv.at[t], sibling
        )

    def has(d, p, k):
        return 1 <= k < half or (k == half and d == p)

    def reduce_scatter(first, tail):
        def compute(k):
            for t in targets(k):
                if first:
                    load(t, other).wait()
                sib_out[t] = partial(t, other).astype(jnp.bfloat16)
                rs_sib(t).start()
            for s, t in enumerate(targets(k)):
                if first:
                    load(t, core).wait()
                part[k % 2, s] = partial(t, core)

        compute(half)
        for k in range(half, 0, -1):
            ts = targets(k)
            for t in ts:
                rs_sib(t).wait_recv()
            for p in range(2):
                for d in range(2):
                    if not has(d, p, k):
                        continue
                    s = d if len(ts) == 2 else 0
                    piece = pl.ds(p * mh, mh)
                    value = part[k % 2, s, piece, :] + sib_in[ts[s], piece, :].astype(jnp.float32)
                    if has(d, p, k + 1):
                        rs_copy(d, p, k + 1).wait_recv()
                        value = value + ring_in[d, k, piece, :].astype(jnp.float32)
                    ring_out[d, k - 1, piece, :] = value.astype(jnp.bfloat16)
                    rs_copy(d, p, k).start()
            compute(k - 1)
            if first:
                for t in ts:
                    squares(t, other)
                    squares(t, core)
        if first:
            squares(ring, other)
            squares(ring, core)
        tail()
        rs_sib(ring).wait_recv()
        for p in range(2):
            for d in range(2):
                rs_copy(d, p, 1).wait_recv()
        total = part[0, 0] + sib_in[ring].astype(jnp.float32)
        for d in range(2):
            total = total + ring_in[d, 0].astype(jnp.float32)
        for k in stages:
            for t in targets(k):
                rs_sib(t).wait_send()
            for p in range(2):
                for d in range(2):
                    if has(d, p, k):
                        rs_copy(d, p, k).wait_send()
        return total

    def ex_copy(e, source, dev):
        return remote(
            totals_out.at[e], totals_in.at[e, source], ex_send.at[e, dev], ex_recv.at[e, source], dev
        )

    def exchange_start(e, row):
        totals_out[e] = jnp.broadcast_to(row, totals_out.shape[1:])

        def body(i, carry):
            ex_copy(e, me, (me + i) % n).start()
            return carry

        lax.fori_loop(1, n, body, 0)

    def exchange_wait(e):
        def body(i, total):
            source = (me + i) % n
            ex_copy(e, source, source).wait()
            return total + totals_in[e, source]

        return lax.fori_loop(1, n, body, totals_out[e])[0:1, :]

    def ag_copy(d, p, h, r):
        piece = gath.at[r, core, pl.ds(p * mh, mh), :]
        return remote(piece, piece, ag_send.at[d, p, h], ag_recv.at[d, p, h], toward[d])

    def ag_sib(r, c, p):
        piece = gath.at[r, c, pl.ds(p * mh, mh), :]
        return remote(piece, piece, agsib_send.at[r, p], agsib_recv.at[r, p], sibling)

    def ag_has(d, p, h):
        return 0 <= h < half - 1 or (h == half - 1 and d == p)

    def all_gather():
        gath[ring, core] = paths[...].astype(jnp.bfloat16)
        for p in range(2):
            for d in range(2):
                ag_copy(d, p, 0, ring).start()
        for p in range(2):
            ag_sib(ring, core, p).start()
        scores[...] = jnp.zeros_like(scores)
        gram[...] = jnp.zeros_like(gram)

        def multiply(r, c):
            block = gath[r, c]
            cols = pl.ds(columns(r, c), width)
            scores[...] += lax.dot_general(
                block, refs[:, cols], NT, preferred_element_type=jnp.float32
            )
            gram[...] += lax.dot_general(block, block, NT, preferred_element_type=jnp.float32)

        def multiply_all(k):
            for t in targets(k):
                multiply(t, core)
            for t in targets(k):
                for p in range(2):
                    ag_sib(t, other, p).wait_recv()
                multiply(t, other)

        for h in range(half):
            for p in range(2):
                for d in range(2):
                    if not ag_has(d, p, h):
                        continue
                    source = at(ring - 1 - h) if d == 0 else at(ring + 1 + h)
                    ag_copy(d, p, h, source).wait_recv()
                    if ag_has(d, p, h + 1):
                        ag_copy(d, p, h + 1, source).start()
                    ag_sib(source, core, p).start()
            multiply_all(h)
        multiply_all(half)
        for h in range(half):
            for p in range(2):
                for d in range(2):
                    if ag_has(d, p, h):
                        ag_copy(d, p, h, at(ring - h) if d == 0 else at(ring + h)).wait_send()
        for k in stages:
            for t in targets(k):
                for p in range(2):
                    ag_sib(t, core, p).wait_send()

    seeded = reduce_scatter(True, lambda: None)
    paths[...] = 0.6 * seeded + 0.8 * noise_ref[...]
    ref_sq = jnp.sum(sq_acc[...].T, axis=0, keepdims=True)
    exchange_start(0, jnp.broadcast_to(jnp.sum(ref_sq, axis=1, keepdims=True), (1, m)))
    sq_acc[0:8, :] = jnp.zeros((8, 128), jnp.float32)
    for j in range(rows // 128):
        sq_acc[j : j + 1, :] = ref_sq[:, j * 128 : (j + 1) * 128]

    def step(e, carry):
        all_gather()

        @pl.when(e == 1)
        def _():
            total = exchange_wait(0) / all_refs
            sq_acc[8:16, :] = jnp.broadcast_to(total, (8, 128))

        scale = sq_acc[8:9, 0:1]
        g = gram[...]
        diag = g * eye
        sq_col = jnp.sum(diag, axis=1, keepdims=True)
        sq_row = jnp.sum(diag, axis=0, keepdims=True)
        sums = jnp.zeros((m, 1), jnp.float32)
        for j in range(rows // 128):
            js = slice(j * 128, (j + 1) * 128)
            w = jnp.exp(
                SHARP
                * (2.0 * scale - sq_col - sq_acc[j : j + 1, :] + 2.0 * scores[:, js])
                / scale
            )
            sums = sums + jnp.sum(w, axis=1, keepdims=True)
            weightb[:, js] = w.astype(jnp.bfloat16)
        exchange_start(e, jnp.sum(eye * sums, axis=0, keepdims=True))

        def tail():
            mutual = jnp.exp(SHARP * (2.0 * scale - sq_col - sq_row + 2.0 * g) / scale) * (1.0 - eye)
            mutual_sum = jnp.sum(mutual, axis=1, keepdims=True)
            totals = jnp.sum(eye * exchange_wait(e), axis=1, keepdims=True)
            now = paths[...]
            pushed = jnp.dot(
                mutual, now, precision=lax.Precision.HIGHEST, preferred_element_type=jnp.float32
            )
            base[...] = (
                now
                + STEP_RATE / m * (mutual_sum * now - pushed)
                - STEP_RATE / all_refs * totals * now
            )

        pulled = reduce_scatter(False, tail)
        paths[...] = base[...] + STEP_RATE / all_refs * pulled
        return carry

    lax.fori_loop(1, STEPS + 1, step, 0)
    out_ref[...] = paths[...]


def shards(n, references, noise, init_idx):
    rows, depth = references.shape
    m, width = noise.shape
    chips, half = n // 2, n // 4
    dma = pltpu.SemaphoreType.DMA
    bf16, f32 = jnp.bfloat16, jnp.float32
    vmem = pl.BlockSpec(memory_space=pltpu.VMEM)
    flops = 2 * m * rows * depth * (2 * STEPS + 1)
    return pl.pallas_call(
        functools.partial(kernel, n),
        out_shape=jax.ShapeDtypeStruct((m, width), f32),
        in_specs=[vmem, vmem, pl.BlockSpec(memory_space=pl.ANY)],
        out_specs=vmem,
        scratch_shapes=[
            pltpu.VMEM((rows, depth), bf16),
            pltpu.VMEM((chips, 2, m, width), bf16),
            pltpu.VMEM((chips, m, width), bf16),
            pltpu.VMEM((chips, m, width), bf16),
            pltpu.VMEM((2, half, m, width), bf16),
            pltpu.VMEM((2, half, m, width), bf16),
            pltpu.VMEM((2, 2, m, width), f32),
            pltpu.VMEM((m, width), f32),
            pltpu.VMEM((m, width), f32),
            pltpu.VMEM((rows, 128), f32),
            pltpu.VMEM((m, rows), f32),
            pltpu.VMEM((m, m), f32),
            pltpu.VMEM((m, rows), bf16),
            pltpu.VMEM((STEPS + 1, 8, m), f32),
            pltpu.VMEM((STEPS + 1, n, 8, m), f32),
            dma((n,)),
            dma((2, 2, half)),
            dma((2, 2, half)),
            dma((chips, 2)),
            dma((chips, 2)),
            dma((2, 2, half)),
            dma((2, 2, half)),
            dma((chips,)),
            dma((chips,)),
            dma((STEPS + 1, n)),
            dma((STEPS + 1, n)),
        ],
        compiler_params=pltpu.CompilerParams(
            collective_id=0, has_side_effects=True, vmem_limit_bytes=56 * 1024 * 1024
        ),
        cost_estimate=pl.CostEstimate(
            flops=flops, bytes_accessed=2 * rows * depth, transcendentals=m * rows * STEPS
        ),
    )(init_idx.reshape(m, 1), noise, references)


def solution(mesh):
    in_specs = (P(("grp", "ref"), None), P("grp", "ref"), P("grp"))
    out_specs = P("grp", "ref")
    return jax.shard_map(
        functools.partial(shards, mesh.shape["ref"]),
        mesh=mesh, in_specs=in_specs, out_specs=out_specs, check_vma=False,
    )
```

```python
import functools

import jax
import jax.numpy as jnp
from jax import lax
from jax.experimental import pallas as pl
from jax.experimental.pallas import tpu as pltpu
from jax.sharding import PartitionSpec as P

STEPS = 2
SHARP = 7.0
STEP_RATE = 0.025
MESH = pl.DeviceIdType.MESH
NT = (((1,), (1,)), ((), ()))


def kernel(
    n, idx_ref, noise_ref, refs_hbm, out_ref,
    refs, gath, sib_out, sib_in, ring_out, ring_in, part, paths, base,
    sq_acc, scores, gram, weightb, totals_out, totals_in,
    load_sem, ag_send, ag_recv, agsib_send, agsib_recv,
    rs_send, rs_recv, rssib_send, rssib_recv, ex_send, ex_recv,
):
    chips, half = n // 2, n // 4
    m, width = noise_ref.shape
    rows = refs.shape[0]
    mh = m // 2
    all_refs = rows * n
    me = lax.axis_index("ref")
    chip, core = me // 2, me % 2
    other = 1 - core

    if n == 16:
        ring = chip // 2 + (chip % 2) * (chips - 1 - 2 * (chip // 2))

        def chip_at(r):
            back = r // half
            return back * (2 * (chips - 1 - r) + 1) + (1 - back) * 2 * r
    else:
        ring = chip

        def chip_at(r):
            return r

    def at(r):
        return (r + chips) % chips

    def pos(r, c):
        return chip_at(r) * 2 + c

    right = pos(at(ring + 1), core)
    left = pos(at(ring - 1), core)
    sibling = chip * 2 + other
    toward = (right, left)
    order = ((0, 0), (1, 1), (0, 1), (1, 0))

    def columns(r, c):
        return pl.multiple_of(pos(r, c) * width, width)

    def remote(src, dst, send, recv, dev):
        return pltpu.make_async_remote_copy(
            src_ref=src, dst_ref=dst, send_sem=send, recv_sem=recv,
            device_id={"ref": dev}, device_id_type=MESH,
        )

    def load(r, c):
        cols = pl.ds(columns(r, c), width)
        return pltpu.make_async_copy(
            refs_hbm.at[:, cols], refs.at[:, cols], load_sem.at[r * 2 + c]
        )

    stages = [half] + list(range(half - 1, 0, -1)) + [0]

    def targets(k):
        if k == 0 or k == half:
            return [at(ring + k)]
        return [at(ring + k), at(ring - k)]

    def start_loads(k):
        for t in targets(k):
            load(t, other).start()
            load(t, core).start()

    start_loads(half)
    start_loads(half - 1)

    barrier = pltpu.get_barrier_semaphore()

    def greet(i, carry):
        pl.semaphore_signal(
            barrier, inc=1, device_id={"ref": (me + i) % n}, device_id_type=MESH
        )
        return carry

    lax.fori_loop(1, n, greet, 0)

    sq_acc[...] = jnp.zeros_like(sq_acc)
    eye = (
        lax.broadcasted_iota(jnp.int32, (m, m), 0) == lax.broadcasted_iota(jnp.int32, (m, m), 1)
    ).astype(jnp.float32)
    offset = jnp.broadcast_to(idx_ref[...] - me * rows, (m, m)).astype(jnp.float32)
    offset = jnp.sum(eye * offset, axis=1, keepdims=True)
    lanes = lax.broadcasted_iota(jnp.int32, (m, rows), 1).astype(jnp.float32)
    weightb[...] = (lanes == offset).astype(jnp.float32).astype(jnp.bfloat16)
    pl.semaphore_wait(barrier, n - 1)

    def partial(r, c):
        cols = pl.ds(columns(r, c), width)
        return jnp.dot(weightb[...], refs[:, cols], preferred_element_type=jnp.float32)

    def squares(r, c):
        start = columns(r, c)
        chunk = 64

        def body(i, carry):
            rs = pl.ds(pl.multiple_of(i * chunk, chunk), chunk)
            total = sq_acc[rs, :]
            for j in range(width // 128):
                x = refs[rs, pl.ds(pl.multiple_of(start + j * 128, 128), 128)].astype(jnp.float32)
                total = total + x * x
            sq_acc[rs, :] = total
            return carry

        lax.fori_loop(0, rows // chunk, body, 0)

    def rs_copy(d, p, k):
        piece = pl.ds(p * mh, mh)
        return remote(
            ring_out.at[d, k - 1, piece, :], ring_in.at[d, k - 1, piece, :],
            rs_send.at[d, p, k - 1], rs_recv.at[d, p, k - 1], toward[d],
        )

    def rs_sib(t):
        return remote(
            sib_out.at[t], sib_in.at[t], rssib_send.at[t], rssib_recv.at[t], sibling
        )

    def has(d, p, k):
        return 1 <= k < half or (k == half and d == p)

    def reduce_scatter(first, head, tail):
        def compute(k):
            for t in targets(k):
                if first:
                    load(t, other).wait()
                sib_out[t] = partial(t, other).astype(jnp.bfloat16)
                rs_sib(t).start()
            for s, t in enumerate(targets(k)):
                if first:
                    load(t, core).wait()
                part[k % 2, s] = partial(t, core)

        compute(half)
        for k in range(half, 0, -1):
            ts = targets(k)
            for t in ts:
                rs_sib(t).wait_recv()
            for d, p in order[2:] + order[:2]:
                if not has(d, p, k):
                    continue
                s = d if len(ts) == 2 else 0
                piece = pl.ds(p * mh, mh)
                value = part[k % 2, s, piece, :] + sib_in[ts[s], piece, :].astype(jnp.float32)
                if has(d, p, k + 1):
                    rs_copy(d, p, k + 1).wait_recv()
                    value = value + ring_in[d, k, piece, :].astype(jnp.float32)
                ring_out[d, k - 1, piece, :] = value.astype(jnp.bfloat16)
                rs_copy(d, p, k).start()
            if first and k >= 2:
                start_loads(k - 2)
            if k == half:
                head()
            compute(k - 1)
            if first:
                for t in ts:
                    squares(t, other)
                    squares(t, core)
        if first:
            squares(ring, other)
            squares(ring, core)
        tail()
        rs_sib(ring).wait_recv()
        for p in range(2):
            for d in range(2):
                rs_copy(d, p, 1).wait_recv()
        total = part[0, 0] + sib_in[ring].astype(jnp.float32)
        for d in range(2):
            total = total + ring_in[d, 0].astype(jnp.float32)
        for k in stages:
            for t in targets(k):
                rs_sib(t).wait_send()
            for p in range(2):
                for d in range(2):
                    if has(d, p, k):
                        rs_copy(d, p, k).wait_send()
        return total

    def ex_copy(e, source, dev):
        return remote(
            totals_out.at[e], totals_in.at[e, source], ex_send.at[e, dev], ex_recv.at[e, source], dev
        )

    def exchange_start(e, row):
        totals_out[e] = jnp.broadcast_to(row, totals_out.shape[1:])

        def body(i, carry):
            ex_copy(e, me, (me + i) % n).start()
            return carry

        lax.fori_loop(1, n, body, 0)

    def exchange_wait(e):
        def body(i, total):
            source = (me + i) % n
            ex_copy(e, source, source).wait()
            return total + totals_in[e, source]

        return lax.fori_loop(1, n, body, totals_out[e])[0:1, :]

    def ag_copy(d, p, h, r):
        piece = gath.at[r, core, pl.ds(p * mh, mh), :]
        return remote(piece, piece, ag_send.at[d, p, h], ag_recv.at[d, p, h], toward[d])

    def ag_sib(r, c, p):
        piece = gath.at[r, c, pl.ds(p * mh, mh), :]
        return remote(piece, piece, agsib_send.at[r, p], agsib_recv.at[r, p], sibling)

    def ag_has(d, p, h):
        return 0 <= h < half - 1 or (h == half - 1 and d == p)

    def all_gather(before_last):
        gath[ring, core] = paths[...].astype(jnp.bfloat16)
        for d, p in order:
            ag_copy(d, p, 0, ring).start()
        for p in range(2):
            ag_sib(ring, core, p).start()
        scores[...] = jnp.zeros_like(scores)
        gram[...] = jnp.zeros_like(gram)

        def multiply(r, c):
            block = gath[r, c]
            cols = pl.ds(columns(r, c), width)
            scores[...] += lax.dot_general(
                block, refs[:, cols], NT, preferred_element_type=jnp.float32
            )
            gram[...] += lax.dot_general(block, block, NT, preferred_element_type=jnp.float32)

        def multiply_all(k):
            for t in targets(k):
                multiply(t, core)
            for t in targets(k):
                for p in range(2):
                    ag_sib(t, other, p).wait_recv()
                multiply(t, other)

        for h in range(half):
            multiply_all(h)
            if h == half - 1:
                before_last()
            for d, p in order:
                if not ag_has(d, p, h):
                    continue
                source = at(ring - 1 - h) if d == 0 else at(ring + 1 + h)
                ag_copy(d, p, h, source).wait_recv()
                if ag_has(d, p, h + 1):
                    ag_copy(d, p, h + 1, source).start()
                ag_sib(source, core, p).start()
        multiply_all(half)
        for h in range(half):
            for p in range(2):
                for d in range(2):
                    if ag_has(d, p, h):
                        ag_copy(d, p, h, at(ring - h) if d == 0 else at(ring + h)).wait_send()
        for k in stages:
            for t in targets(k):
                for p in range(2):
                    ag_sib(t, core, p).wait_send()

    seeded = reduce_scatter(True, lambda: None, lambda: None)
    paths[...] = 0.6 * seeded + 0.8 * noise_ref[...]
    ref_sq = jnp.sum(sq_acc[...].T, axis=0, keepdims=True)
    exchange_start(0, jnp.broadcast_to(jnp.sum(ref_sq, axis=1, keepdims=True), (1, m)))
    sq_acc[0:8, :] = jnp.zeros((8, 128), jnp.float32)
    for j in range(rows // 128):
        sq_acc[j : j + 1, :] = ref_sq[:, j * 128 : (j + 1) * 128]

    def step(e, carry):
        def before_last():
            @pl.when(e == 1)
            def _():
                total = exchange_wait(0) / all_refs
                sq_acc[8:16, :] = jnp.broadcast_to(total, (8, 128))

        all_gather(before_last)

        scale = sq_acc[8:9, 0:1]
        g = gram[...]
        diag = g * eye
        sq_col = jnp.sum(diag, axis=1, keepdims=True)
        sq_row = jnp.sum(diag, axis=0, keepdims=True)
        sums = jnp.zeros((m, 1), jnp.float32)
        for j in range(rows // 128):
            js = slice(j * 128, (j + 1) * 128)
            w = jnp.exp(
                SHARP
                * (2.0 * scale - sq_col - sq_acc[j : j + 1, :] + 2.0 * scores[:, js])
                / scale
            )
            sums = sums + jnp.sum(w, axis=1, keepdims=True)
            weightb[:, js] = w.astype(jnp.bfloat16)

        def head():
            exchange_start(e, jnp.sum(eye * sums, axis=0, keepdims=True))

        def tail():
            mutual = jnp.exp(SHARP * (2.0 * scale - sq_col - sq_row + 2.0 * g) / scale) * (1.0 - eye)
            mutual_sum = jnp.sum(mutual, axis=1, keepdims=True)
            totals = jnp.sum(eye * exchange_wait(e), axis=1, keepdims=True)
            now = paths[...]
            pushed = jnp.dot(
                mutual, now, precision=lax.Precision.HIGHEST, preferred_element_type=jnp.float32
            )
            base[...] = (
                now
                + STEP_RATE / m * (mutual_sum * now - pushed)
                - STEP_RATE / all_refs * totals * now
            )

        pulled = reduce_scatter(False, head, tail)
        paths[...] = base[...] + STEP_RATE / all_refs * pulled
        return carry

    lax.fori_loop(1, STEPS + 1, step, 0)
    out_ref[...] = paths[...]


def shards(n, references, noise, init_idx):
    rows, depth = references.shape
    m, width = noise.shape
    chips, half = n // 2, n // 4
    dma = pltpu.SemaphoreType.DMA
    bf16, f32 = jnp.bfloat16, jnp.float32
    vmem = pl.BlockSpec(memory_space=pltpu.VMEM)
    flops = 2 * m * rows * depth * (2 * STEPS + 1)
    return pl.pallas_call(
        functools.partial(kernel, n),
        out_shape=jax.ShapeDtypeStruct((m, width), f32),
        in_specs=[vmem, vmem, pl.BlockSpec(memory_space=pl.ANY)],
        out_specs=vmem,
        scratch_shapes=[
            pltpu.VMEM((rows, depth), bf16),
            pltpu.VMEM((chips, 2, m, width), bf16),
            pltpu.VMEM((chips, m, width), bf16),
            pltpu.VMEM((chips, m, width), bf16),
            pltpu.VMEM((2, half, m, width), bf16),
            pltpu.VMEM((2, half, m, width), bf16),
            pltpu.VMEM((2, 2, m, width), f32),
            pltpu.VMEM((m, width), f32),
            pltpu.VMEM((m, width), f32),
            pltpu.VMEM((rows, 128), f32),
            pltpu.VMEM((m, rows), f32),
            pltpu.VMEM((m, m), f32),
            pltpu.VMEM((m, rows), bf16),
            pltpu.VMEM((STEPS + 1, 8, m), f32),
            pltpu.VMEM((STEPS + 1, n, 8, m), f32),
            dma((n,)),
            dma((2, 2, half)),
            dma((2, 2, half)),
            dma((chips, 2)),
            dma((chips, 2)),
            dma((2, 2, half)),
            dma((2, 2, half)),
            dma((chips,)),
            dma((chips,)),
            dma((STEPS + 1, n)),
            dma((STEPS + 1, n)),
        ],
        compiler_params=pltpu.CompilerParams(
            collective_id=0, has_side_effects=True, vmem_limit_bytes=56 * 1024 * 1024
        ),
        cost_estimate=pl.CostEstimate(
            flops=flops, bytes_accessed=2 * rows * depth, transcendentals=m * rows * STEPS
        ),
    )(init_idx.reshape(1, m), noise, references)


def solution(mesh):
    in_specs = (P(("grp", "ref"), None), P("grp", "ref"), P("grp"))
    out_specs = P("grp", "ref")
    return jax.shard_map(
        functools.partial(shards, mesh.shape["ref"]),
        mesh=mesh, in_specs=in_specs, out_specs=out_specs, check_vma=False,
    )
```
